1024 devices in a mesh: dp: 4 (over y_hi), row: 8 (over x, core), col: 32 (over y_lo, z).
Axes of the slice: x: 4, y: 8 (y_hi: 4, y_lo: 2; y = y_hi * 2 + y_lo), z: 16, core: 2. Of those that a mesh axis runs over, the one named last changes fastest.
Arguments:
- grad_out: bfloat16 [1024, 8192], P(('dp', 'col'), 'row'), may hold values from -6 to 6
- saved_hidden: bfloat16 [1024, 26624], P(('dp', 'row'), 'col'), may hold values from -0.1875 to 0.1875
- down_weight: bfloat16 [26624, 8192], P('col', 'row'), may hold values from -0.0625 to 0.0625
Outputs:
- input_grad: bfloat16 [1024, 26624], P(('dp', 'row'), 'col')
- weight_grad: bfloat16 [26624, 8192], P(('col', 'dp'), 'row')
The draws below stay inside these ranges and needn't reach their ends.
All inputs are finite; a program needn't handle non-finite values.
Results may differ from the reference program's by a relative error of at most 0.001.
Values may be sent and summed in bfloat16 or wider, within the bound.
A program may use at most 32 MiB of HBM per device.

```python
import jax
import jax.numpy as jnp

D = 8192
FFW = 26624
TOKENS = 1024


def block_levels(stream_key, extent, pieces, least, largest):
    factor_of = 1.0
    for axis_at, shards_of in pieces:
        heights = jax.random.uniform(jax.random.fold_in(jax.random.fold_in(stream_key, 6), axis_at), (shards_of,), jnp.float32, least / len(pieces), largest / len(pieces))
        factor_of = factor_of * jnp.repeat(jnp.exp(heights), extent[axis_at] // shards_of).reshape((-1,) + (1,) * (len(extent) - 1 - axis_at))
    return factor_of


def noise(own_key, dims, spread, most, pieces=(), held_as=jnp.bfloat16):
    entries = jax.random.normal(own_key, dims, jnp.float32) * spread
    if len(pieces) > 0:
        entries = block_levels(own_key, dims, pieces, -0.22, 0.18) * entries
    return jnp.clip(entries, min=-most, max=most).astype(held_as)


def setup_inputs(seed: int = 0) -> dict:
    keys = jax.random.split(jax.random.key(seed), 4)
    return {
        "grad_out": noise(keys[0], (TOKENS, D), 1.0, 6.0, ((0, 128), (1, 8))),
        "saved_hidden": noise(keys[1], (TOKENS, FFW), (TOKENS ** -0.5), 0.1875, ((0, 32), (1, 32))),
        "down_weight": noise(keys[2], (FFW, D), D ** -0.5, 0.0625, ((0, 32), (1, 8))),
    }


def reference(grad_out, saved_hidden, down_weight):
    input_grad = jnp.dot(grad_out, down_weight.T, preferred_element_type=jnp.float32).astype(jnp.bfloat16)
    weight_grad = jnp.dot(saved_hidden.T, grad_out, preferred_element_type=jnp.float32).astype(jnp.bfloat16)
    return input_grad, weight_grad
```

```python
import functools

import jax
import jax.numpy as jnp
from jax import lax
from jax.experimental import pallas as pl
from jax.experimental.pallas import tpu as pltpu
from jax.sharding import PartitionSpec as P

MESH = pl.DeviceIdType.MESH
F32, BF16 = jnp.float32, jnp.bfloat16
LAG = 1


def rel_of(slot, n):
    return (-(slot + 1) // 2 if slot % 2 else slot // 2) % n


def groups_of(n):
    return [(0, 1)] + [(2 * g - 1, 2) for g in range(1, n // 2)] + [(n - 1, 1)]


def kernel(nx, ny, nz, g_hbm, h_hbm, w_hbm, ig_ref, wg_ref, gb, hv, hs, hb, ht, wv, ps, pr, rr, acc,
           lsem, zs, zr, ys, yr, hss, hrs, iss, irs):
    ndp = ny // 2
    hid = h_hbm.shape[1]
    quarter = hid // ndp
    tg, cols = g_hbm.shape
    th = h_hbm.shape[0]
    dp, row, col = (lax.axis_index(a) for a in ("dp", "row", "col"))
    y, z = dp * 2 + lax.div(col, nz), lax.rem(col, nz)
    y_lo = lax.div(col, nz)
    x, c = lax.div(row, 2), lax.rem(row, 2)

    def at(x_=None, y_=None, z_=None, c_=None):
        xx = x if x_ is None else lax.rem(x + x_ + nx, nx)
        yy = y if y_ is None else lax.rem(y + y_ + ny, ny)
        zz = z if z_ is None else lax.rem(z + z_ + nz, nz)
        cc = c if c_ is None else 1 - c
        return (lax.div(yy, 2), xx * 2 + cc, lax.rem(yy, 2) * nz + zz)

    load_g = pltpu.make_async_copy(g_hbm, gb.at[0, 0], lsem.at[0])
    load_h = pltpu.make_async_copy(h_hbm, hv, lsem.at[1])
    load_w = pltpu.make_async_copy(w_hbm, wv, lsem.at[2])
    load_g.start()
    load_h.start()
    load_w.start()
    barrier = pltpu.get_barrier_semaphore()
    peers = (
        [at(z_=d) for d in range(1, nz)]
        + [at(y_=d) for d in sorted({1, ny - 1} | set(range(2, ny, 2)))]
        + [at(x_=d) for d in range(1, nx)]
        + [at(c_=1)]
    )
    for p in peers:
        pl.semaphore_signal(barrier, inc=1, device_id=p, device_id_type=MESH)
    load_h.wait()
    hs[...] = jnp.zeros_like(hs)
    for k in range(ndp):
        hs[k, :, :quarter] = hv[:, k * quarter:(k + 1) * quarter]
    load_g.wait()
    pl.semaphore_wait(barrier, len(peers))

    def remote(src, dst, ss, rs, to):
        return pltpu.make_async_remote_copy(src_ref=src, dst_ref=dst, send_sem=ss, recv_sem=rs, device_id=to, device_id_type=MESH)

    sent = []

    zc = {}
    for s in range(1, nz):
        zc[s] = remote(gb.at[0, 0], gb.at[0, s], zs.at[s], zr.at[s], at(z_=-rel_of(s, nz) % nz))
    zgroups = groups_of(nz)
    ng = len(zgroups)
    top = ny // 2

    def y_copy(up, level, g):
        s0, n = zgroups[g]
        if level == top:
            if n == 2:
                s0, n = s0 + (0 if up else 1), 1
            elif (g == 0) != up:
                return None
        frm = 0 if level == 1 else (2 * level - 3 if up else 2 * level - 2)
        to = ny - 1 if level == top else (2 * level - 1 if up else 2 * level)
        k = ((level - 1) * 2 + (0 if up else 1)) * ng + g
        return remote(gb.at[frm, pl.ds(s0, n)], gb.at[to, pl.ds(s0, n)], ys.at[k], yr.at[k], at(y_=1 if up else -1))

    yc = {(u, l, g): y_copy(u, l, g) for u in (True, False) for l in range(1, top + 1) for g in range(ng)}

    def send(cp):
        if cp is not None:
            cp.start()
            sent.append(cp)

    def y_send(level, g):
        for u in (True, False):
            send(yc[u, level, g])

    y_send(1, 0)
    for s in range(1, nz):
        send(zc[s])
    h1 = []
    for j, d in enumerate(range(2, ny, 2)):
        to_dp = lax.rem(dp + d // 2, ndp)
        h1.append(remote(hs.at[to_dp], hb.at[row, dp], hss.at[j], hrs.at[j], at(y_=d)))
        send(h1[-1])
    hb[row, dp] = hs[dp]
    h2 = [remote(hb.at[row], hb.at[row], hss.at[ndp + j], hrs.at[ndp + j], at(x_=d)) for j, d in enumerate(range(1, nx))]
    h3 = []
    for j in range(nx):
        r = lax.rem(x + nx - j, nx) * 2 + c
        k = ndp + nx + j
        h3.append(remote(hb.at[r], hb.at[r], hss.at[k], hrs.at[k], at(c_=1)))

    def do_h2():
        for cp in h1:
            cp.wait_recv()
        for cp in h2:
            send(cp)
        send(h3[0])

    def do_h3():
        for j, cp in enumerate(h2):
            cp.wait_recv()
            send(h3[j + 1])

    def do_ht():
        for cp in h3:
            cp.wait_recv()
        tok = nz * tg
        a = lax.broadcasted_iota(jnp.int32, (tok, tok), 0)
        b = lax.broadcasted_iota(jnp.int32, (tok, tok), 1)
        slot = lax.div(b, tg)
        half = lax.div(slot + 1, 2)
        rel = jnp.where(lax.rem(slot, 2) == 1, nz - half, half)
        want = lax.rem(z + rel, nz) * tg + lax.rem(b, tg)
        perm = jnp.where(a == want, 1.0, 0.0).astype(BF16)
        nr = tok // th
        for o in range(ny):
            yy = lax.rem(y + rel_of(o, ny), ny)
            blk = hb[pl.ds(lax.rem(yy, 2) * nr, nr), lax.div(yy, 2)].reshape(tok, hs.shape[2])
            got = lax.dot_general(blk, perm, (((0,), (0,)), ((), ())), preferred_element_type=F32)
            ht[o] = got.astype(BF16)

    def partial(block, of_y):
        xg = gb[block].reshape(nz * tg, cols)
        p = lax.dot_general(xg, wv[...], (((1,), (1,)), ((), ())), preferred_element_type=F32)
        per = th // tg
        for s in range(nz):
            za = lax.rem(z + rel_of(s, nz), nz)
            r = of_y * (nz // per) + lax.div(za, per)
            ps[lax.rem(r, 2), lax.div(r, 2), lax.rem(za, per)] = p[s * tg:(s + 1) * tg]

    r1 = remote(ps.at[1 - c], pr, iss.at[0], irs.at[0], at(c_=1))
    r2 = []
    for j, d in enumerate(range(1, nx)):
        r2.append(remote(pr.at[lax.rem(x + d, nx)], rr.at[j], iss.at[1 + j], irs.at[1 + j], at(x_=d)))

    def do_own():
        load_w.wait()
        partial(0, y_lo)

    def do_pair():
        partial(jnp.where(y_lo == 0, 2, 1) if top > 1 else 1, 1 - y_lo)
        send(r1)

    def do_r2():
        r1.wait_recv()
        for j, d in enumerate(range(1, nx)):
            k = lax.rem(x + d, nx)
            pr[k] = pr[k] + ps[c, k]
            send(r2[j])

    def do_r3():
        total = pr[x] + ps[c, x]
        for j, cp in enumerate(r2):
            cp.wait_recv()
            total = total + rr[j]
        ig_ref[...] = total.reshape(th, hid).astype(BF16)

    def weight(lo, hi, first):
        t = None
        for o in range(lo, hi):
            d = jnp.dot(ht[o], gb[o].reshape(nz * tg, cols), preferred_element_type=F32)
            t = d if t is None else t + d
        t = t[:quarter]
        return t if first else acc[...] + t

    def z_step(g):
        s0, n = zgroups[g]
        if g:
            for s in range(s0, s0 + n):
                zc[s].wait_recv()
            y_send(1, g)

    def y_step(level, g):
        for u in (True, False):
            if yc[u, level, g] is not None:
                yc[u, level, g].wait_recv()
        if level < top:
            y_send(level + 1, g)

    rounds = ng + LAG * top
    done = set()
    for r in range(rounds + 1):
        if r < ng:
            z_step(r)
        for level in range(1, top):
            g = r - LAG * level
            if 0 <= g < ng:
                y_step(level, g)
        if r == 2:
            do_h2()
        if r == 4:
            do_h3()
        if r == 5:
            do_ht()
        if r == ng - 1:
            do_own()
        if r == ng - 1 + LAG:
            do_pair()
        if r == ng + 2 * LAG:
            do_r2()
    cut = 2 * min(2, top - 1) + 1
    acc[...] = weight(0, cut, True)
    do_r3()
    for g in range(ng):
        y_step(top, g)
    wg_ref[...] = weight(cut, ny, False).astype(BF16)
    for cp in sent:
        cp.wait_send()


def local(nx, ny, nz, grad_out, saved_hidden, down_weight):
    tg, cols = grad_out.shape
    th, hid = saved_hidden.shape
    ndp = ny // 2
    quarter = hid // ndp
    wide = -(-quarter // 128) * 128
    top = ny // 2
    nyc = 2 * top * (nz // 2 + 1)
    dma = pltpu.SemaphoreType.DMA
    return pl.pallas_call(
        functools.partial(kernel, nx, ny, nz),
        out_shape=(jax.ShapeDtypeStruct((th, hid), BF16), jax.ShapeDtypeStruct((quarter, cols), BF16)),
        in_specs=[pl.BlockSpec(memory_space=pl.ANY)] * 3,
        out_specs=(pl.BlockSpec(memory_space=pltpu.VMEM),) * 2,
        scratch_shapes=[
            pltpu.VMEM((ny, nz, tg, cols), BF16),
            pltpu.VMEM((th, hid), BF16),
            pltpu.VMEM((ndp, th, wide), BF16),
            pltpu.VMEM((2 * nx, ndp, th, wide), BF16),
            pltpu.VMEM((ny, wide, nz * tg), BF16),
            pltpu.VMEM(down_weight.shape, BF16),
            pltpu.VMEM((2, nx, th // tg, tg, hid), F32),
            pltpu.VMEM((nx, th // tg, tg, hid), F32),
            pltpu.VMEM((nx - 1, th // tg, tg, hid), F32),
            pltpu.VMEM((quarter, cols), F32),
            dma((3,)), dma((nz,)), dma((nz,)), dma((nyc,)), dma((nyc,)),
            dma((ndp + 2 * nx,)), dma((ndp + 2 * nx,)), dma((nx,)), dma((nx,)),
        ],
        compiler_params=pltpu.CompilerParams(collective_id=0, has_side_effects=True, vmem_limit_bytes=48 << 20),
        name="mlp_grads",
    )(grad_out, saved_hidden, down_weight)


def solution(mesh):
    nx, ny, nz = mesh.shape["row"] // 2, mesh.shape["dp"] * 2, mesh.shape["col"] // 2
    placed = (P(("dp", "col"), "row"), P(("dp", "row"), "col"), P("col", "row"))
    return jax.shard_map(
        functools.partial(local, nx, ny, nz),
        mesh=mesh,
        in_specs=placed,
        out_specs=(P(("dp", "row"), "col"), P(("col", "dp"), "row")),
        check_vma=False,
    )
```

```python
import functools

import jax
import jax.numpy as jnp
from jax import lax
from jax.experimental import pallas as pl
from jax.experimental.pallas import tpu as pltpu
from jax.sharding import PartitionSpec as P

MESH = pl.DeviceIdType.MESH
F32, BF16 = jnp.float32, jnp.bfloat16
LAG = 3
H_AT = (0, 3, 6, 8)
SEND = {0: [(2, 3)], 1: [(0, 1), (1, 2)], 2: [(1, 3)], 3: [(0, 2), (0, 3)]}
FROM = {0: [0], 1: [1], 3: [2, 3]}
NEAR = 4
Z_FIRST = False


def rel_of(slot, n):
    return (-((slot + 1) // 2) if slot % 2 else slot // 2) % n


def kernel(nx, ny, nz, g_hbm, h_hbm, w_hbm, ig_ref, wg_ref, gb, hv, hs, hb, ht, wv, ps, pr, mine, rr, acc,
           lsem, zs, zr, ys, yr, hss, hrs, iss, irs, in_z, in_o):
    ndp = ny // 2
    hid = h_hbm.shape[1]
    quarter = hid // ndp
    tg, cols = g_hbm.shape
    th = h_hbm.shape[0]
    per = th // tg
    nq = nz // per
    size = 2 if per % 2 == 0 else 1
    ng = nz // size
    top = ny // 2
    dp, row, col = (lax.axis_index(a) for a in ("dp", "row", "col"))
    y_lo, z = lax.div(col, nz), lax.rem(col, nz)
    y = dp * 2 + y_lo
    x, c = lax.div(row, 2), lax.rem(row, 2)

    def dev(x_=None, y_=None, z_=None, c_=None):
        xx, yy = (x if x_ is None else x_), (y if y_ is None else y_)
        zz, cc = (z if z_ is None else z_), (c if c_ is None else c_)
        return (lax.div(yy, 2), xx * 2 + cc, lax.rem(yy, 2) * nz + zz)

    def signal(sem, to):
        pl.semaphore_signal(sem, inc=1, device_id=to, device_id_type=MESH)

    def wait(sem, n):
        @pl.when(n > 0)
        def _():
            pl.semaphore_wait(sem, n)

    def remote(src, dst, ss, rs, to):
        return pltpu.make_async_remote_copy(src_ref=src, dst_ref=dst, send_sem=ss, recv_sem=rs, device_id=to, device_id_type=MESH)

    def up(d):
        return lax.rem(y + d, ny)

    y_near = sorted({1, ny - 1})
    y_far = list(range(2, ny, 2))
    peers = [(dev(y_=up(d)), up(d) > y, 0) for d in y_near] + [(dev(y_=up(d)), up(d) > y, 1) for d in y_far]
    peers += [(dev(x_=lax.rem(x + d, nx)), lax.rem(x + d, nx) > x, 2) for d in range(1, nx)]
    peers += [(dev(c_=1 - c), c == 0, 3)]

    load_g = pltpu.make_async_copy(g_hbm, gb.at[0, z], lsem.at[0])
    load_h = pltpu.make_async_copy(h_hbm, hv, lsem.at[1])
    load_w = pltpu.make_async_copy(w_hbm, wv, lsem.at[2])
    load_g.start()
    load_h.start()
    load_w.start()
    barrier = pltpu.get_barrier_semaphore()
    run, place = lax.div(z, NEAR), lax.rem(z, NEAR)
    before = jnp.int32(0)
    is_near = [jnp.logical_and(run == k // NEAR, k != z) for k in range(nz)]
    is_far = [jnp.logical_and(place == k % NEAR, k != z) for k in range(nz)]
    is_peer = [jnp.logical_or(n, f) for n, f in zip(is_near, is_far)]
    for k in range(nz):
        pl.when(jnp.logical_and(is_peer[k], k > z))(functools.partial(signal, barrier, dev(z_=k)))
        before = before + jnp.where(jnp.logical_and(is_peer[k], k < z), 1, 0)
    later = [0, 0, 0, 0]
    for to, is_later, kind in peers:
        pl.when(is_later)(functools.partial(signal, barrier, to))
        n = jnp.where(is_later, 1, 0)
        before = before + 1 - n
        later[kind] = later[kind] + n
    load_h.wait()
    hs[...] = jnp.zeros_like(hs)
    for k in range(ndp):
        hs[k, :, :quarter] = hv[:, k * quarter:(k + 1) * quarter]
    hb[row, dp] = hs[dp]
    load_g.wait()
    wait(barrier, before)

    def z_copy(k, to, sem):
        return remote(gb.at[0, k], gb.at[0, k], zs.at[sem], zr.at[k], dev(z_=to))

    def near_sem(to, k):
        return lax.rem(to, NEAR) * (nz // NEAR) + lax.div(k, NEAR)

    def far_sem(to):
        return nz + to // NEAR

    def to_earlier(k):
        signal(in_z.at[z], dev(z_=k))

        @pl.when(is_near[k])
        def _():
            z_copy(z, k, near_sem(k, z)).start()

        @pl.when(is_far[k])
        def _():
            z_copy(z, k, far_sem(k)).start()

    for k in range(nz):
        pl.when(jnp.logical_and(is_peer[k], k < z))(functools.partial(to_earlier, k))
    for to, is_later, kind in peers:
        pl.when(jnp.logical_not(is_later))(functools.partial(signal, in_o.at[kind], to))

    def y_copy(up_, level, g):
        s0, n = g * size, size
        if level == top:
            if n == 1:
                if (g % 2 == 0) != up_:
                    return None
            else:
                s0, n = s0 + (0 if up_ else 1), 1
        frm = 0 if level == 1 else (2 * level - 3 if up_ else 2 * level - 2)
        to = ny - 1 if level == top else (2 * level - 1 if up_ else 2 * level)
        k = ((level - 1) * 2 + (0 if up_ else 1)) * ng + g
        return remote(gb.at[frm, pl.ds(s0, n)], gb.at[to, pl.ds(s0, n)], ys.at[k], yr.at[k], dev(y_=up(1 if up_ else ny - 1)))

    yc = {(u, l, g): y_copy(u, l, g) for u in (True, False) for l in range(1, top + 1) for g in range(ng)}
    sent = []

    def send(cp):
        if cp is not None:
            cp.start()
            sent.append(cp)

    def y_send(level, g):
        for u in (True, False):
            send(yc[u, level, g])

    h1 = []
    for j, d in enumerate(y_far):
        to_dp = lax.rem(dp + d // 2, ndp)
        h1.append(remote(hs.at[to_dp], hb.at[row, dp], hss.at[j], hrs.at[j], dev(y_=up(d))))
    h2 = [remote(hb.at[row], hb.at[row], hss.at[ndp + j], hrs.at[ndp + j], dev(x_=lax.rem(x + d, nx)))
          for j, d in enumerate(range(1, nx))]
    h3 = []
    for j in range(nx):
        r = lax.rem(x + nx - j, nx) * 2 + c
        k = ndp + nx + j
        h3.append(remote(hb.at[r], hb.at[r], hss.at[k], hrs.at[k], dev(c_=1 - c)))

    def do_h1():
        wait(in_o.at[1], later[1])
        for cp in h1:
            send(cp)

    def do_h2():
        for cp in h1:
            cp.wait_recv()
        wait(in_o.at[2], later[2])
        for cp in h2:
            send(cp)
        wait(in_o.at[3], later[3])
        send(h3[0])

    def do_h3():
        for j, cp in enumerate(h2):
            cp.wait_recv()
            send(h3[j + 1])

    def do_ht():
        for cp in h3:
            cp.wait_recv()
        for q in range(nq):
            parts = []
            for o in range(ny):
                yy = up(rel_of(o, ny))
                parts.append(hb[lax.rem(yy, 2) * nq + q, lax.div(yy, 2)])
            ht[q] = jnp.concatenate(parts, 0).T

    def partial(q):
        own = gb[0, per * q:per * (q + 1)].reshape(th, cols)
        other = gb[jnp.where(y_lo == 0, 2, 1) if top > 1 else 1, per * q:per * (q + 1)].reshape(th, cols)
        xg = jnp.concatenate([own, other], 0)
        p = lax.dot_general(xg, wv[...], (((1,), (1,)), ((), ())), preferred_element_type=F32)
        ps[q, y_lo] = p[:th]
        ps[q, 1 - y_lo] = p[th:]

    r1 = [remote(ps.at[q], pr.at[q // 2], iss.at[q], irs.at[q], dev(c_=1 - c)) for q in range(nq)]

    def r2_of(q, half):
        to_x = half * (nx // 2) + q // 2
        j = lax.rem(x - to_x + nx, nx) - 1
        return to_x, remote(pr.at[q // 2, half], rr.at[j], iss.at[nq + (q // 2) * 2 + half], irs.at[nq + j], dev(x_=to_x))

    def do_partial(q):
        partial(q)
        pl.when(c != q % 2)(r1[q].start)

    def do_sum(q):
        @pl.when(c == q % 2)
        def _():
            r1[q].wait_recv()
            for half in range(2):
                to_x, cp = r2_of(q, half)
                pr[q // 2, half] = pr[q // 2, half] + ps[q, half]

                @pl.when(x != to_x)
                def _():
                    cp.start()

                @pl.when(x == to_x)
                def _():
                    mine[...] = pr[q // 2, half]

    def do_total():
        total = mine[...]
        for j in range(nx - 1):
            remote(rr.at[j], rr.at[j], iss.at[j], irs.at[nq + j], dev(c_=1 - c)).wait_recv()
            total = total + rr[j]
        ig_ref[...] = total.astype(BF16)

    def do_weight(q):
        blk = gb[:, per * q:per * (q + 1)].reshape(ny * th, cols)
        t = jnp.dot(ht[q], blk, preferred_element_type=F32)[:quarter]
        if q:
            t = acc[...] + t
        if q < nq - 1:
            acc[...] = t
        else:
            wg_ref[...] = t.astype(BF16)

    def to_later_near(p):
        @pl.when(jnp.logical_and(is_near[p], p > z))
        def _():
            pl.semaphore_wait(in_z.at[p], 1)
            z_copy(z, p, near_sem(p, z)).start()

    def to_later_run(of, to):
        @pl.when(run == of)
        def _():
            p = to * NEAR + place
            pl.semaphore_wait(in_z.at[p], 1)
            z_copy(z, p, nz + to).start()

    def from_run(r):
        @pl.when(run != r)
        def _():
            k = r * NEAR + place
            z_copy(k, z, 0).wait_recv()
            for m in range(NEAR):
                p = run * NEAR + m

                @pl.when(m != place)
                def _():
                    z_copy(k, p, near_sem(p, k)).start()

    def z_step(g):
        if g == 0:
            for p in range(nz):
                to_later_near(p)
        for of, to in SEND.get(g, ()):
            to_later_run(of, to)
        for r in FROM.get(g, ()):
            from_run(r)
        for k in range(g * size, (g + 1) * size):
            @pl.when(jnp.logical_and(k != z, jnp.logical_not(is_far[k])))
            def _():
                z_copy(k, z, 0).wait_recv()
        if g == 0:
            wait(in_o.at[0], later[0])
        y_send(1, g)

    def y_step(level, g):
        for u in (True, False):
            if yc[u, level, g] is not None:
                yc[u, level, g].wait_recv()
        if level < top:
            y_send(level + 1, g)

    gq = per // size
    todo = {}

    def plan(r, f, *a):
        todo.setdefault(r, []).append(functools.partial(f, *a))

    for r, f in zip(H_AT, (do_h1, do_h2, do_h3, do_ht)):
        plan(r, f)
    plan(0, load_w.wait)
    for q in range(nq):
        last = (q + 1) * gq - 1
        plan(last + LAG, do_partial, q)
        plan(last + LAG + 1, do_sum, q)
        plan(last + LAG * top + (q < nq - 1), do_weight, q)
    plan(ng + LAG * top, do_total)
    for r in range(ng + LAG * top + 1):
        def zz():
            if r < ng:
                z_step(r)
        if Z_FIRST:
            zz()
        for level in range(1, top + 1):
            g = r - LAG * level
            if 0 <= g < ng:
                y_step(level, g)
        if not Z_FIRST:
            zz()
        for f in todo.pop(r, []):
            f()
    assert not todo
    for cp in sent:
        cp.wait_send()
    for p in range(nz):
        @pl.when(is_near[p])
        def _():
            for r in range(nz // NEAR):
                k = r * NEAR + place
                z_copy(k, p, near_sem(p, k)).wait_send()

        @pl.when(is_far[p])
        def _():
            z_copy(z, p, far_sem(p)).wait_send()
    for q in range(nq):
        pl.when(c != q % 2)(r1[q].wait_send)
        for half in range(2):
            to_x, cp = r2_of(q, half)
            pl.when(jnp.logical_and(c == q % 2, x != to_x))(cp.wait_send)


def local(nx, ny, nz, grad_out, saved_hidden, down_weight):
    tg, cols = grad_out.shape
    th, hid = saved_hidden.shape
    ndp = ny // 2
    quarter = hid // ndp
    wide = -(-quarter // 128) * 128
    nq = nz // (th // tg)
    nyc = 2 * (ny // 2) * nz
    dma, reg = pltpu.SemaphoreType.DMA, pltpu.SemaphoreType.REGULAR
    return pl.pallas_call(
        functools.partial(kernel, nx, ny, nz),
        out_shape=(jax.ShapeDtypeStruct((th, hid), BF16), jax.ShapeDtypeStruct((quarter, cols), BF16)),
        in_specs=[pl.BlockSpec(memory_space=pltpu.HBM)] * 3,
        out_specs=(pl.BlockSpec(memory_space=pltpu.VMEM),) * 2,
        scratch_shapes=[
            pltpu.VMEM((ny, nz, tg, cols), BF16),
            pltpu.VMEM((th, hid), BF16),
            pltpu.VMEM((ndp, th, wide), BF16),
            pltpu.VMEM((2 * nx, ndp, th, wide), BF16),
            pltpu.VMEM((nq, wide, ny * th), BF16),
            pltpu.VMEM(down_weight.shape, BF16),
            pltpu.VMEM((nq, 2, th, hid), F32),
            pltpu.VMEM((nq // 2, 2, th, hid), F32),
            pltpu.VMEM((th, hid), F32),
            pltpu.VMEM((nx - 1, th, hid), F32),
            pltpu.VMEM((quarter, cols), F32),
            dma((3,)), dma((nz + nz // NEAR,)), dma((nz,)), dma((nyc,)), dma((nyc,)),
            dma((ndp + 2 * nx,)), dma((ndp + 2 * nx,)), dma((2 * nq,)), dma((2 * nq,)),
            reg((nz,)), reg((4,)),
        ],
        compiler_params=pltpu.CompilerParams(collective_id=0, has_side_effects=True, vmem_limit_bytes=53 << 20),
        name="mlp_grads",
    )(grad_out, saved_hidden, down_weight)


def solution(mesh):
    nx, ny, nz = mesh.shape["row"] // 2, mesh.shape["dp"] * 2, mesh.shape["col"] // 2
    placed = (P(("dp", "col"), "row"), P(("dp", "row"), "col"), P("col", "row"))
    return jax.shard_map(
        functools.partial(local, nx, ny, nz),
        mesh=mesh,
        in_specs=placed,
        out_specs=(P(("dp", "row"), "col"), P(("col", "dp"), "row")),
        check_vma=False,
    )
```

```python
import functools

import jax
import jax.numpy as jnp
from jax import lax
from jax.experimental import pallas as pl
from jax.experimental.pallas import tpu as pltpu
from jax.sharding import PartitionSpec as P

MESH = pl.DeviceIdType.MESH
F32, BF16 = jnp.float32, jnp.bfloat16
LAG = 4
H_AT = (0, 3, 6, 9)
SEND = {0: [(2, 3)], 1: [(0, 1), (1, 2)], 2: [(1, 3), (0, 2), (0, 3)]}
FROM = {0: [0], 1: [1], 2: [2], 3: [3]}
NEAR = 4
Z_FIRST = False


def rel_of(slot, n):
    return (-((slot + 1) // 2) if slot % 2 else slot // 2) % n


def kernel(nx, ny, nz, g_hbm, h_hbm, w_hbm, ig_ref, wg_ref, gb, hv, hs, hb, ht, wv, ps, pr, mine, rr, acc,
           lsem, zs, zr, ys, yr, hss, hrs, iss, irs, in_z, in_o):
    ndp = ny // 2
    hid = h_hbm.shape[1]
    quarter = hid // ndp
    tg, cols = g_hbm.shape
    th = h_hbm.shape[0]
    per = th // tg
    nq = nz // per
    size = 2 if per % 2 == 0 else 1
    ng = nz // size
    top = ny // 2
    dp, row, col = (lax.axis_index(a) for a in ("dp", "row", "col"))
    y_lo, z = lax.div(col, nz), lax.rem(col, nz)
    y = dp * 2 + y_lo
    x, c = lax.div(row, 2), lax.rem(row, 2)

    def dev(x_=None, y_=None, z_=None, c_=None):
        xx, yy = (x if x_ is None else x_), (y if y_ is None else y_)
        zz, cc = (z if z_ is None else z_), (c if c_ is None else c_)
        return (lax.div(yy, 2), xx * 2 + cc, lax.rem(yy, 2) * nz + zz)

    def signal(sem, to):
        pl.semaphore_signal(sem, inc=1, device_id=to, device_id_type=MESH)

    def wait(sem, n):
        @pl.when(n > 0)
        def _():
            pl.semaphore_wait(sem, n)

    def remote(src, dst, ss, rs, to):
        return pltpu.make_async_remote_copy(src_ref=src, dst_ref=dst, send_sem=ss, recv_sem=rs, device_id=to, device_id_type=MESH)

    def up(d):
        return lax.rem(y + d, ny)

    y_near = sorted({1, ny - 1})
    y_far = list(range(2, ny, 2))
    peers = [(dev(y_=up(d)), up(d) > y, 0) for d in y_near] + [(dev(y_=up(d)), up(d) > y, 1) for d in y_far]
    peers += [(dev(x_=lax.rem(x + d, nx)), lax.rem(x + d, nx) > x, 2) for d in range(1, nx)]
    peers += [(dev(c_=1 - c), c == 0, 3)]

    load_g = pltpu.make_async_copy(g_hbm, gb.at[0, z], lsem.at[0])
    load_h = pltpu.make_async_copy(h_hbm, hv, lsem.at[1])
    load_w = pltpu.make_async_copy(w_hbm, wv, lsem.at[2])
    load_g.start()
    load_h.start()
    load_w.start()
    barrier = pltpu.get_barrier_semaphore()
    run, place = lax.div(z, NEAR), lax.rem(z, NEAR)
    before = jnp.int32(0)
    is_near = [jnp.logical_and(run == k // NEAR, k != z) for k in range(nz)]
    is_far = [jnp.logical_and(place == k % NEAR, k != z) for k in range(nz)]
    is_peer = [jnp.logical_or(n, f) for n, f in zip(is_near, is_far)]
    for k in range(nz):
        pl.when(jnp.logical_and(is_peer[k], k > z))(functools.partial(signal, barrier, dev(z_=k)))
        before = before + jnp.where(jnp.logical_and(is_peer[k], k < z), 1, 0)
    later = [0, 0, 0, 0]
    for to, is_later, kind in peers:
        pl.when(is_later)(functools.partial(signal, barrier, to))
        n = jnp.where(is_later, 1, 0)
        before = before + 1 - n
        later[kind] = later[kind] + n
    load_h.wait()
    hs[...] = jnp.zeros_like(hs)
    for k in range(ndp):
        hs[k, :, :quarter] = hv[:, k * quarter:(k + 1) * quarter]
    hb[row, dp] = hs[dp]
    load_g.wait()
    wait(barrier, before)

    def z_copy(k, to, sem):
        return remote(gb.at[0, k], gb.at[0, k], zs.at[sem], zr.at[k], dev(z_=to))

    def near_sem(to, k):
        return lax.rem(to, NEAR) * (nz // NEAR) + lax.div(k, NEAR)

    def far_sem(to):
        return nz + to // NEAR

    def to_earlier(k):
        signal(in_z.at[z], dev(z_=k))

        @pl.when(is_near[k])
        def _():
            z_copy(z, k, near_sem(k, z)).start()

        @pl.when(is_far[k])
        def _():
            z_copy(z, k, far_sem(k)).start()

    for k in range(nz):
        pl.when(jnp.logical_and(is_peer[k], k < z))(functools.partial(to_earlier, k))
    for to, is_later, kind in peers:
        pl.when(jnp.logical_not(is_later))(functools.partial(signal, in_o.at[kind], to))

    def y_copy(up_, level, g):
        s0, n = g * size, size
        if level == top:
            if n == 1:
                if (g % 2 == 0) != up_:
                    return None
            else:
                s0, n = s0 + (0 if up_ else 1), 1
        frm = 0 if level == 1 else (2 * level - 3 if up_ else 2 * level - 2)
        to = ny - 1 if level == top else (2 * level - 1 if up_ else 2 * level)
        k = ((level - 1) * 2 + (0 if up_ else 1)) * ng + g
        return remote(gb.at[frm, pl.ds(s0, n)], gb.at[to, pl.ds(s0, n)], ys.at[k], yr.at[k], dev(y_=up(1 if up_ else ny - 1)))

    yc = {(u, l, g): y_copy(u, l, g) for u in (True, False) for l in range(1, top + 1) for g in range(ng)}
    sent = []

    def send(cp):
        if cp is not None:
            cp.start()
            sent.append(cp)

    def y_send(level, g):
        for u in (True, False):
            send(yc[u, level, g])

    h1 = []
    for j, d in enumerate(y_far):
        to_dp = lax.rem(dp + d // 2, ndp)
        h1.append(remote(hs.at[to_dp], hb.at[row, dp], hss.at[j], hrs.at[j], dev(y_=up(d))))
    h2 = [remote(hb.at[row], hb.at[row], hss.at[ndp + j], hrs.at[ndp + j], dev(x_=lax.rem(x + d, nx)))
          for j, d in enumerate(range(1, nx))]
    h3 = []
    for j in range(nx):
        r = lax.rem(x + nx - j, nx) * 2 + c
        k = ndp + nx + j
        h3.append(remote(hb.at[r], hb.at[r], hss.at[k], hrs.at[k], dev(c_=1 - c)))

    def do_h1():
        wait(in_o.at[1], later[1])
        for cp in h1:
            send(cp)

    def do_h2():
        for cp in h1:
            cp.wait_recv()
        wait(in_o.at[2], later[2])
        for cp in h2:
            send(cp)
        wait(in_o.at[3], later[3])
        send(h3[0])

    def do_h3():
        for j, cp in enumerate(h2):
            cp.wait_recv()
            send(h3[j + 1])

    def do_ht():
        for cp in h3:
            cp.wait_recv()
        for q in range(nq):
            parts = []
            for o in range(ny):
                yy = up(rel_of(o, ny))
                parts.append(hb[lax.rem(yy, 2) * nq + q, lax.div(yy, 2)])
            ht[q] = jnp.concatenate(parts, 0).T

    def partial(q):
        own = gb[0, per * q:per * (q + 1)].reshape(th, cols)
        other = gb[jnp.where(y_lo == 0, 2, 1) if top > 1 else 1, per * q:per * (q + 1)].reshape(th, cols)
        xg = jnp.concatenate([own, other], 0)
        p = lax.dot_general(xg, wv[...], (((1,), (1,)), ((), ())), preferred_element_type=F32)
        ps[q, y_lo] = p[:th]
        ps[q, 1 - y_lo] = p[th:]

    r1 = [remote(ps.at[q], pr.at[q // 2], iss.at[q], irs.at[q], dev(c_=1 - c)) for q in range(nq)]

    def r2_of(q, half):
        to_x = half * (nx // 2) + q // 2
        j = lax.rem(x - to_x + nx, nx) - 1
        return to_x, remote(pr.at[q // 2, half], rr.at[j], iss.at[nq + (q // 2) * 2 + half], irs.at[nq + j], dev(x_=to_x))

    def do_partial(q):
        partial(q)
        pl.when(c != q % 2)(r1[q].start)

    def do_sum(q):
        @pl.when(c == q % 2)
        def _():
            r1[q].wait_recv()
            for half in range(2):
                to_x, cp = r2_of(q, half)
                pr[q // 2, half] = pr[q // 2, half] + ps[q, half]

                @pl.when(x != to_x)
                def _():
                    cp.start()

                @pl.when(x == to_x)
                def _():
                    mine[...] = pr[q // 2, half]

    def do_total():
        total = mine[...]
        for j in range(nx - 1):
            remote(rr.at[j], rr.at[j], iss.at[j], irs.at[nq + j], dev(c_=1 - c)).wait_recv()
            total = total + rr[j]
        ig_ref[...] = total.astype(BF16)

    def do_weight(q):
        blk = gb[:, per * q:per * (q + 1)].reshape(ny * th, cols)
        t = jnp.dot(ht[q], blk, preferred_element_type=F32)[:quarter]
        if q:
            t = acc[...] + t
        if q < nq - 1:
            acc[...] = t
        else:
            wg_ref[...] = t.astype(BF16)

    def to_later_near(p):
        @pl.when(jnp.logical_and(is_near[p], p > z))
        def _():
            pl.semaphore_wait(in_z.at[p], 1)
            z_copy(z, p, near_sem(p, z)).start()

    def to_later_run(of, to):
        @pl.when(run == of)
        def _():
            p = to * NEAR + place
            pl.semaphore_wait(in_z.at[p], 1)
            z_copy(z, p, nz + to).start()

    def from_run(r):
        @pl.when(run != r)
        def _():
            k = r * NEAR + place
            z_copy(k, z, 0).wait_recv()
            for m in range(NEAR):
                p = run * NEAR + m

                @pl.when(m != place)
                def _():
                    z_copy(k, p, near_sem(p, k)).start()

    def z_step(g):
        if g == 0:
            for p in range(nz):
                to_later_near(p)
        for of, to in SEND.get(g, ()):
            to_later_run(of, to)
        for r in FROM.get(g, ()):
            from_run(r)
        for k in range(g * size, (g + 1) * size):
            @pl.when(jnp.logical_and(k != z, jnp.logical_not(is_far[k])))
            def _():
                z_copy(k, z, 0).wait_recv()
        if g == 0:
            wait(in_o.at[0], later[0])
        y_send(1, g)

    def y_step(level, g):
        for u in (True, False):
            if yc[u, level, g] is not None:
                yc[u, level, g].wait_recv()
        if level < top:
            y_send(level + 1, g)

    gq = per // size
    todo = {}

    def plan(r, f, *a):
        todo.setdefault(r, []).append(functools.partial(f, *a))

    for r, f in zip(H_AT, (do_h1, do_h2, do_h3, do_ht)):
        plan(r, f)
    plan(0, load_w.wait)
    for q in range(nq):
        last = (q + 1) * gq - 1
        plan(last + LAG, do_partial, q)
        plan(last + LAG + 1, do_sum, q)
        plan(last + LAG * top + (q < nq - 1), do_weight, q)
    plan(ng + LAG * top, do_total)
    for r in range(ng + LAG * top + 1):
        def zz():
            if r < ng:
                z_step(r)
        if Z_FIRST:
            zz()
        for level in range(1, top + 1):
            g = r - LAG * level
            if 0 <= g < ng:
                y_step(level, g)
        if not Z_FIRST:
            zz()
        for f in todo.pop(r, []):
            f()
    assert not todo
    for cp in sent:
        cp.wait_send()
    for p in range(nz):
        @pl.when(is_near[p])
        def _():
            for r in range(nz // NEAR):
                k = r * NEAR + place
                z_copy(k, p, near_sem(p, k)).wait_send()

        @pl.when(is_far[p])
        def _():
            z_copy(z, p, far_sem(p)).wait_send()
    for q in range(nq):
        pl.when(c != q % 2)(r1[q].wait_send)
        for half in range(2):
            to_x, cp = r2_of(q, half)
            pl.when(jnp.logical_and(c == q % 2, x != to_x))(cp.wait_send)


def local(nx, ny, nz, grad_out, saved_hidden, down_weight):
    tg, cols = grad_out.shape
    th, hid = saved_hidden.shape
    ndp = ny // 2
    quarter = hid // ndp
    wide = -(-quarter // 128) * 128
    nq = nz // (th // tg)
    nyc = 2 * (ny // 2) * nz
    dma, reg = pltpu.SemaphoreType.DMA, pltpu.SemaphoreType.REGULAR
    return pl.pallas_call(
        functools.partial(kernel, nx, ny, nz),
        out_shape=(jax.ShapeDtypeStruct((th, hid), BF16), jax.ShapeDtypeStruct((quarter, cols), BF16)),
        in_specs=[pl.BlockSpec(memory_space=pltpu.HBM)] * 3,
        out_specs=(pl.BlockSpec(memory_space=pltpu.VMEM),) * 2,
        scratch_shapes=[
            pltpu.VMEM((ny, nz, tg, cols), BF16),
            pltpu.VMEM((th, hid), BF16),
            pltpu.VMEM((ndp, th, wide), BF16),
            pltpu.VMEM((2 * nx, ndp, th, wide), BF16),
            pltpu.VMEM((nq, wide, ny * th), BF16),
            pltpu.VMEM(down_weight.shape, BF16),
            pltpu.VMEM((nq, 2, th, hid), F32),
            pltpu.VMEM((nq // 2, 2, th, hid), F32),
            pltpu.VMEM((th, hid), F32),
            pltpu.VMEM((nx - 1, th, hid), F32),
            pltpu.VMEM((quarter, cols), F32),
            dma((3,)), dma((nz + nz // NEAR,)), dma((nz,)), dma((nyc,)), dma((nyc,)),
            dma((ndp + 2 * nx,)), dma((ndp + 2 * nx,)), dma((2 * nq,)), dma((2 * nq,)),
            reg((nz,)), reg((4,)),
        ],
        compiler_params=pltpu.CompilerParams(collective_id=0, has_side_effects=True, vmem_limit_bytes=53 << 20),
        name="mlp_grads",
    )(grad_out, saved_hidden, down_weight)


def solution(mesh):
    nx, ny, nz = mesh.shape["row"] // 2, mesh.shape["dp"] * 2, mesh.shape["col"] // 2
    placed = (P(("dp", "col"), "row"), P(("dp", "row"), "col"), P("col", "row"))
    return jax.shard_map(
        functools.partial(local, nx, ny, nz),
        mesh=mesh,
        in_specs=placed,
        out_specs=(P(("dp", "row"), "col"), P(("col", "dp"), "row")),
        check_vma=False,
    )
```

```python
import functools

import jax
import jax.numpy as jnp
from jax import lax
from jax.experimental import pallas as pl
from jax.experimental.pallas import tpu as pltpu
from jax.sharding import PartitionSpec as P

MESH = pl.DeviceIdType.MESH
F32, BF16 = jnp.float32, jnp.bfloat16
LAG = 4
H_AT = (0, 3, 6, 9)
SEND = {0: [(2, 3)], 1: [(0, 1), (1, 2)], 2: [(1, 3), (0, 2), (0, 3)]}
FROM = {0: [0], 1: [1], 2: [2], 3: [3]}
NEAR = 4
Z_FIRST = False


def rel_of(slot, n):
    return (-((slot + 1) // 2) if slot % 2 else slot // 2) % n


def kernel(nx, ny, nz, g_hbm, h_hbm, w_hbm, ig_ref, wg_ref, gb, hv, hs, hb, ht, wv, ps, pr, mine, rr, acc,
           lsem, zs, zr, ys, yr, hss, hrs, iss, irs, in_z, in_o):
    ndp = ny // 2
    hid = h_hbm.shape[1]
    quarter = hid // ndp
    tg, cols = g_hbm.shape
    th = h_hbm.shape[0]
    per = th // tg
    nq = nz // per
    size = 2 if per % 2 == 0 else 1
    ng = nz // size
    top = ny // 2
    dp, row, col = (lax.axis_index(a) for a in ("dp", "row", "col"))
    y_lo, z = lax.div(col, nz), lax.rem(col, nz)
    y = dp * 2 + y_lo
    x, c = lax.div(row, 2), lax.rem(row, 2)

    def dev(x_=None, y_=None, z_=None, c_=None):
        xx, yy = (x if x_ is None else x_), (y if y_ is None else y_)
        zz, cc = (z if z_ is None else z_), (c if c_ is None else c_)
        return (lax.div(yy, 2), xx * 2 + cc, lax.rem(yy, 2) * nz + zz)

    def signal(sem, to):
        pl.semaphore_signal(sem, inc=1, device_id=to, device_id_type=MESH)

    def wait(sem, n):
        @pl.when(n > 0)
        def _():
            pl.semaphore_wait(sem, n)

    def remote(src, dst, ss, rs, to):
        return pltpu.make_async_remote_copy(src_ref=src, dst_ref=dst, send_sem=ss, recv_sem=rs, device_id=to, device_id_type=MESH)

    def up(d):
        return lax.rem(y + d, ny)

    y_near = sorted({1, ny - 1})
    y_far = list(range(2, ny, 2))
    peers = [(dev(y_=up(d)), up(d) > y, 0) for d in y_near] + [(dev(y_=up(d)), up(d) > y, 1) for d in y_far]
    peers += [(dev(x_=lax.rem(x + d, nx)), lax.rem(x + d, nx) > x, 2) for d in range(1, nx)]
    peers += [(dev(c_=1 - c), c == 0, 3)]

    load_g = pltpu.make_async_copy(g_hbm, gb.at[0, z], lsem.at[0])
    load_h = pltpu.make_async_copy(h_hbm, hv, lsem.at[1])
    load_w = pltpu.make_async_copy(w_hbm, wv, lsem.at[2])
    load_g.start()
    load_h.start()
    load_w.start()
    barrier = pltpu.get_barrier_semaphore()
    run, place = lax.div(z, NEAR), lax.rem(z, NEAR)
    before = jnp.int32(0)
    is_near = [jnp.logical_and(run == k // NEAR, k != z) for k in range(nz)]
    is_far = [jnp.logical_and(place == k % NEAR, k != z) for k in range(nz)]
    is_peer = [jnp.logical_or(n, f) for n, f in zip(is_near, is_far)]
    for k in range(nz):
        pl.when(jnp.logical_and(is_peer[k], k > z))(functools.partial(signal, barrier, dev(z_=k)))
        before = before + jnp.where(jnp.logical_and(is_peer[k], k < z), 1, 0)
    later = [0, 0, 0, 0]
    for to, is_later, kind in peers:
        pl.when(is_later)(functools.partial(signal, barrier, to))
        n = jnp.where(is_later, 1, 0)
        before = before + 1 - n
        later[kind] = later[kind] + n
    load_h.wait()
    hs[...] = jnp.zeros_like(hs)
    for k in range(ndp):
        hs[k, :, :quarter] = hv[:, k * quarter:(k + 1) * quarter]
    hb[row, dp] = hs[dp]
    load_g.wait()
    wait(barrier, before)

    def z_copy(k, to, sem):
        return remote(gb.at[0, k], gb.at[0, k], zs.at[sem], zr.at[k], dev(z_=to))

    def near_sem(to, k):
        return lax.rem(to, NEAR) * (nz // NEAR) + lax.div(k, NEAR)

    def far_sem(to):
        return nz + to // NEAR

    def to_earlier(k):
        signal(in_z.at[z], dev(z_=k))

        @pl.when(is_near[k])
        def _():
            z_copy(z, k, near_sem(k, z)).start()

        @pl.when(is_far[k])
        def _():
            z_copy(z, k, far_sem(k)).start()

    for k in range(nz):
        pl.when(jnp.logical_and(is_peer[k], k < z))(functools.partial(to_earlier, k))
    for to, is_later, kind in peers:
        pl.when(jnp.logical_not(is_later))(functools.partial(signal, in_o.at[kind], to))

    def y_copy(up_, level, g):
        s0, n = g * size, size
        if level == top:
            if n == 1:
                if (g % 2 == 0) != up_:
                    return None
            else:
                s0, n = s0 + (0 if up_ else 1), 1
        frm = 0 if level == 1 else (2 * level - 3 if up_ else 2 * level - 2)
        to = ny - 1 if level == top else (2 * level - 1 if up_ else 2 * level)
        k = ((level - 1) * 2 + (0 if up_ else 1)) * ng + g
        return remote(gb.at[frm, pl.ds(s0, n)], gb.at[to, pl.ds(s0, n)], ys.at[k], yr.at[k], dev(y_=up(1 if up_ else ny - 1)))

    yc = {(u, l, g): y_copy(u, l, g) for u in (True, False) for l in range(1, top + 1) for g in range(ng)}
    sent = []

    def send(cp):
        if cp is not None:
            cp.start()
            sent.append(cp)

    def y_send(level, g):
        for u in (True, False):
            send(yc[u, level, g])

    h1 = []
    for j, d in enumerate(y_far):
        to_dp = lax.rem(dp + d // 2, ndp)
        h1.append(remote(hs.at[to_dp], hb.at[row, dp], hss.at[j], hrs.at[j], dev(y_=up(d))))
    h2 = [remote(hb.at[row], hb.at[row], hss.at[ndp + j], hrs.at[ndp + j], dev(x_=lax.rem(x + d, nx)))
          for j, d in enumerate(range(1, nx))]
    h3 = []
    for j in range(nx):
        r = lax.rem(x + nx - j, nx) * 2 + c
        k = ndp + nx + j
        h3.append(remote(hb.at[r], hb.at[r], hss.at[k], hrs.at[k], dev(c_=1 - c)))

    def do_h1():
        wait(in_o.at[1], later[1])
        for cp in h1:
            send(cp)

    def do_h2():
        for cp in h1:
            cp.wait_recv()
        wait(in_o.at[2], later[2])
        for cp in h2:
            send(cp)
        wait(in_o.at[3], later[3])
        send(h3[0])

    def do_h3():
        for j, cp in enumerate(h2):
            cp.wait_recv()
            send(h3[j + 1])

    def do_ht():
        for cp in h3:
            cp.wait_recv()
        for q in range(nq):
            parts = []
            for o in range(ny):
                yy = up(rel_of(o, ny))
                parts.append(hb[lax.rem(yy, 2) * nq + q, lax.div(yy, 2)])
            ht[q] = jnp.concatenate(parts, 0).T

    def partial(q):
        own = gb[0, per * q:per * (q + 1)].reshape(th, cols)
        other = gb[jnp.where(y_lo == 0, 2, 1) if top > 1 else 1, per * q:per * (q + 1)].reshape(th, cols)
        xg = jnp.concatenate([own, other], 0)
        p = lax.dot_general(xg, wv[...], (((1,), (1,)), ((), ())), preferred_element_type=F32)
        ps[q, y_lo] = p[:th]
        ps[q, 1 - y_lo] = p[th:]

    r1 = [remote(ps.at[q], pr.at[q // 2], iss.at[q], irs.at[q], dev(c_=1 - c)) for q in range(nq)]

    def r2_of(q, half):
        to_x = half * (nx // 2) + q // 2
        j = lax.rem(x - to_x + nx, nx) - 1
        return to_x, remote(pr.at[q // 2, half], rr.at[j], iss.at[nq + (q // 2) * 2 + half], irs.at[nq + j], dev(x_=to_x))

    def do_partial(q):
        partial(q)
        pl.when(c != q % 2)(r1[q].start)

    def do_sum(q):
        @pl.when(c == q % 2)
        def _():
            r1[q].wait_recv()
            for half in range(2):
                to_x, cp = r2_of(q, half)
                pr[q // 2, half] = pr[q // 2, half] + ps[q, half]

                @pl.when(x != to_x)
                def _():
                    cp.start()

                @pl.when(x == to_x)
                def _():
                    mine[...] = pr[q // 2, half]

    def do_total():
        total = mine[...]
        for j in range(nx - 1):
            remote(rr.at[j], rr.at[j], iss.at[j], irs.at[nq + j], dev(c_=1 - c)).wait_recv()
            total = total + rr[j]
        ig_ref[...] = total.astype(BF16)

    def do_weight(q):
        blk = gb[:, per * q:per * (q + 1)].reshape(ny * th, cols)
        t = jnp.dot(ht[q], blk, preferred_element_type=F32)[:quarter]
        if q:
            t = acc[...] + t
        if q < nq - 1:
            acc[...] = t
        else:
            wg_ref[...] = t.astype(BF16)

    def to_later_near(p):
        @pl.when(jnp.logical_and(is_near[p], p > z))
        def _():
            pl.semaphore_wait(in_z.at[p], 1)
            z_copy(z, p, near_sem(p, z)).start()

    def to_later_run(of, to):
        @pl.when(run == of)
        def _():
            p = to * NEAR + place
            pl.semaphore_wait(in_z.at[p], 1)
            z_copy(z, p, nz + to).start()

    def from_run(r):
        @pl.when(run != r)
        def _():
            k = r * NEAR + place
            z_copy(k, z, 0).wait_recv()
            for m in range(NEAR):
                p = run * NEAR + m

                @pl.when(m != place)
                def _():
                    z_copy(k, p, near_sem(p, k)).start()

    def z_step(g):
        if g == 0:
            for p in range(nz):
                to_later_near(p)
        for of, to in SEND.get(g, ()):
            to_later_run(of, to)
        for r in FROM.get(g, ()):
            from_run(r)
        for k in range(g * size, (g + 1) * size):
            @pl.when(jnp.logical_and(k != z, jnp.logical_not(is_far[k])))
            def _():
                z_copy(k, z, 0).wait_recv()
        if g == 0:
            wait(in_o.at[0], later[0])
        y_send(1, g)

    def y_step(level, g):
        for u in (True, False):
            if yc[u, level, g] is not None:
                yc[u, level, g].wait_recv()
        if level < top:
            y_send(level + 1, g)

    gq = per // size
    todo = {}

    def plan(r, f, *a):
        todo.setdefault(r, []).append(functools.partial(f, *a))

    for r, f in zip(H_AT, (do_h1, do_h2, do_h3, do_ht)):
        plan(r, f)
    plan(0, load_w.wait)
    for q in range(nq):
        last = (q + 1) * gq - 1
        plan(last + LAG, do_partial, q)
        plan(last + LAG + 1, do_sum, q)
        plan(last + LAG * top + (q < nq - 1), do_weight, q)
    plan(ng + LAG * top, do_total)
    for r in range(ng + LAG * top + 1):
        def zz():
            if r < ng:
                z_step(r)
        if Z_FIRST:
            zz()
        for level in range(1, top + 1):
            g = r - LAG * level
            if 0 <= g < ng:
                y_step(level, g)
        if not Z_FIRST:
            zz()
        for f in todo.pop(r, []):
            f()
    assert not todo
    for cp in sent:
        cp.wait_send()
    for p in range(nz):
        @pl.when(is_near[p])
        def _():
            for r in range(nz // NEAR):
                k = r * NEAR + place
                z_copy(k, p, near_sem(p, k)).wait_send()

        @pl.when(is_far[p])
        def _():
            z_copy(z, p, far_sem(p)).wait_send()
    for q in range(nq):
        pl.when(c != q % 2)(r1[q].wait_send)
        for half in range(2):
            to_x, cp = r2_of(q, half)
            pl.when(jnp.logical_and(c == q % 2, x != to_x))(cp.wait_send)


def local(nx, ny, nz, grad_out, saved_hidden, down_weight):
    tg, cols = grad_out.shape
    th, hid = saved_hidden.shape
    ndp = ny // 2
    quarter = hid // ndp
    wide = -(-quarter // 128) * 128
    nq = nz // (th // tg)
    nyc = 2 * (ny // 2) * nz
    dma, reg = pltpu.SemaphoreType.DMA, pltpu.SemaphoreType.REGULAR
    return pl.pallas_call(
        functools.partial(kernel, nx, ny, nz),
        out_shape=(pltpu.VMEM((th, hid), BF16), pltpu.VMEM((quarter, cols), BF16)),
        in_specs=[pl.BlockSpec(memory_space=pltpu.HBM)] * 3,
        out_specs=(pl.BlockSpec(memory_space=pltpu.VMEM),) * 2,
        scratch_shapes=[
            pltpu.VMEM((ny, nz, tg, cols), BF16),
            pltpu.VMEM((th, hid), BF16),
            pltpu.VMEM((ndp, th, wide), BF16),
            pltpu.VMEM((2 * nx, ndp, th, wide), BF16),
            pltpu.VMEM((nq, wide, ny * th), BF16),
            pltpu.VMEM(down_weight.shape, BF16),
            pltpu.VMEM((nq, 2, th, hid), F32),
            pltpu.VMEM((nq // 2, 2, th, hid), F32),
            pltpu.VMEM((th, hid), F32),
            pltpu.VMEM((nx - 1, th, hid), F32),
            pltpu.VMEM((quarter, cols), F32),
            dma((3,)), dma((nz + nz // NEAR,)), dma((nz,)), dma((nyc,)), dma((nyc,)),
            dma((ndp + 2 * nx,)), dma((ndp + 2 * nx,)), dma((2 * nq,)), dma((2 * nq,)),
            reg((nz,)), reg((4,)),
        ],
        compiler_params=pltpu.CompilerParams(collective_id=0, has_side_effects=True, vmem_limit_bytes=54 << 20),
        name="mlp_grads",
    )(grad_out, saved_hidden, down_weight)


def solution(mesh):
    nx, ny, nz = mesh.shape["row"] // 2, mesh.shape["dp"] * 2, mesh.shape["col"] // 2
    placed = (P(("dp", "col"), "row"), P(("dp", "row"), "col"), P("col", "row"))
    return jax.shard_map(
        functools.partial(local, nx, ny, nz),
        mesh=mesh,
        in_specs=placed,
        out_specs=(P(("dp", "row"), "col"), P(("col", "dp"), "row")),
        check_vma=False,
    )
```
